32 devices in a mesh: sph: 8 (over z, core), wave: 4 (over y, x).
Axes of the slice: x: 2, y: 2, z: 4, core: 2. Of those that a mesh axis runs over, the one named last changes fastest.
Arguments:
- coefficients: float32 [8, 96, 1024], P(None, None, 'sph'), may hold values from -6 to 6
- incident: float32 [8, 96, 1024], P(None, None, 'sph'), may hold values from -6 to 6
- positions: float32 [3, 1024], P(None, 'sph'), may hold values from 0 to 1
- neighbour_index: int32 [12, 1024], P(None, 'sph'), may hold values from 0 to 1023, as said below
- link_class: int32 [12, 1024], P(None, 'sph'), may hold values from 0 to 25
- link_count: int32 [1024], P('sph'), may hold values from 1 to 12, as said below
- sphere_type: int32 [1024], P('sph'), may hold values from 0 to 3
- translation: float32 [2, 26, 48, 48], replicated, may hold values from -0.1875 to 0.1875
- t_matrix: float32 [2, 4, 48, 48], replicated, may hold values from -0.375 to 0.375
- wave_grid: int32 [2, 2048], P(None, 'wave'), may hold values from -64 to 63
- vertical: float32 [2048], P('wave'), may hold values from 0.5 to 4
- expansion: float32 [2, 2, 48, 2048], P(None, None, None, 'wave'), may hold values from -0.01953125 to 0.01953125
- reflection: float32 [2, 2, 2, 2048], P(None, None, None, 'wave'), may hold values from -3 to 3
- projector: float32 [2, 48, 2, 2048], P(None, None, None, 'wave'), may hold values from -0.046875 to 0.046875
Outputs:
- updated: float32 [8, 96, 1024], P(None, None, 'sph')
The draws below stay inside these ranges and needn't reach their ends.
Inputs may be any that keep to these rules, and one draw needn't show every extreme that they name: `neighbour_index`: every entry lies within 128 of its own sphere's index; slots at or past link_count hold valid indices that are not used. `link_count`: the spheres of some aligned blocks of 128 have many more live slots than others.
All inputs are finite; a program needn't handle non-finite values.
Results may differ from the reference program's by a relative error of at most 0.0003.
Values sent between devices are 32-bit elements; how exact they have to be, the bound alone decides.
A program may use at most 64 MiB of HBM per device.

```python
import math
import jax
import jax.numpy as jnp
from jax import lax

MODES = 48
ILLUMS = 8
LINKS = 12
OFFSETS = 26
TYPES = 4
GRID = 64
SPH_DEV = 128
WAVE_DEV = 512
SPHERES = 1024
WAVES = 2048
N_WAVE = 4


def draw_neighbour_index(key, part):
    spheres = lax.broadcasted_iota(jnp.int32, (LINKS, SPHERES), 1)
    slot_ids = lax.broadcasted_iota(jnp.int32, (LINKS, SPHERES), 0)
    offset = jax.random.randint(jax.random.fold_in(key, 11), (LINKS, SPHERES), -SPH_DEV, SPH_DEV + 1)
    target = jnp.clip(spheres + offset, 0, SPHERES - 1)
    target = jnp.where((slot_ids == 0) & (spheres == SPHERES - 1), SPHERES - 1, target)
    target = jnp.where((slot_ids == 0) & (spheres == 0), 0, target)
    return target.astype(jnp.int32)


def draw_link_count(key, part):
    blocks = SPHERES // SPH_DEV
    block_extra = jax.random.randint(jax.random.fold_in(key, 21), (blocks,), 0, 2 * LINKS)
    base_count = jax.random.randint(jax.random.fold_in(key, 22), (blocks, SPH_DEV), 1, LINKS + 1)
    link_total = jnp.minimum(base_count + block_extra[:, None] // 3, LINKS)
    position = lax.broadcasted_iota(jnp.int32, (blocks, SPH_DEV), 1)
    link_total = jnp.where(position == 0, LINKS, link_total)
    link_total = jnp.where(position == 1, 1, link_total)
    return link_total.reshape(SPHERES).astype(jnp.int32)


def place_ends(entries, own_key, low, top_value):
    index_at = [jax.random.randint(jax.random.fold_in(own_key, axis), (), 0, length) for axis, length in enumerate(entries.shape)]
    widest = entries.shape.index(max(entries.shape))
    next_to = index_at[:widest] + [(index_at[widest] + 1) % entries.shape[widest]] + index_at[widest + 1:]
    return entries.at[tuple(index_at)].set(low).at[tuple(next_to)].set(top_value)


def block_scale(stream_key, dims, cuts, low, top_value):
    factor_of, own = 1.0, jax.random.fold_in(stream_key, 6)
    for dim, blocks in cuts:
        steps = jnp.exp(jax.random.uniform(jax.random.fold_in(own, dim), (blocks,), jnp.float32, low / len(cuts), top_value / len(cuts)))
        factor_of = factor_of * jnp.repeat(steps, dims[dim] // blocks).reshape([-1 if axis == dim else 1 for axis in range(len(dims))])
    return factor_of


def gaussian(stream_key, dims, width, reach, cuts=(), dtype=jnp.bfloat16):
    values = width * jax.random.normal(stream_key, dims, jnp.float32)
    if cuts:
        values = values * block_scale(stream_key, dims, cuts, -0.22, 0.18)
    return jnp.clip(values, -reach, reach).astype(dtype)


def setup_inputs(seed: int = 0) -> dict:
    key_list = jax.random.split(jax.random.key(seed), 15)
    return {
        "coefficients": gaussian(key_list[0], (ILLUMS, 2 * MODES, SPHERES), 1.0, 6.0, ((2, 8),), jnp.float32),
        "incident": gaussian(key_list[1], (ILLUMS, 2 * MODES, SPHERES), 1.0, 6.0, ((2, 8),), jnp.float32),
        "positions": jnp.clip(1.0 * jax.random.uniform(key_list[2], (3, SPHERES), jnp.float32) ** block_scale(key_list[2], (3, SPHERES), ((1, 8),), -0.2, 0.2), 0.0, 1.0),
        "neighbour_index": draw_neighbour_index(jax.random.fold_in(key_list[14], 71), 0),
        "link_class": place_ends(jax.random.randint(key_list[4], (LINKS, SPHERES), 0, OFFSETS), jax.random.fold_in(key_list[4], 1), 0, OFFSETS - 1).astype(jnp.int32),
        "link_count": draw_link_count(jax.random.fold_in(key_list[14], 71), 0),
        "sphere_type": place_ends(jax.random.randint(key_list[6], (SPHERES,), 0, TYPES), jax.random.fold_in(key_list[6], 1), 0, TYPES - 1).astype(jnp.int32),
        "translation": gaussian(key_list[7], (2, OFFSETS, MODES, MODES), (2 * MODES * LINKS) ** -0.5, 0.1875, (), jnp.float32),
        "t_matrix": gaussian(key_list[8], (2, TYPES, MODES, MODES), (6 * MODES) ** -0.5, 0.375, (), jnp.float32),
        "wave_grid": place_ends(jax.random.randint(key_list[9], (2, WAVES), -GRID, GRID), jax.random.fold_in(key_list[9], 1), -GRID, GRID - 1).astype(jnp.int32),
        "vertical": jnp.clip(jnp.exp(math.log(4.0) - 2.0794415 * jax.random.uniform(key_list[10], (WAVES,), jnp.float32) ** block_scale(key_list[10], (WAVES,), ((0, 4),), -0.2, 0.2)), 0.5, 4.0),
        "expansion": gaussian(key_list[11], (2, 2, MODES, WAVES), (2 * MODES * SPHERES) ** -0.5, 0.01953125, ((3, 4),), jnp.float32),
        "reflection": gaussian(key_list[12], (2, 2, 2, WAVES), 0.5, 3.0, ((3, 4),), jnp.float32),
        "projector": gaussian(key_list[13], (2, MODES, 2, WAVES), (8 * WAVES) ** -0.5, 0.046875, ((3, 4),), jnp.float32),
    }


PRECISE = lax.Precision.HIGHEST
TWO_PI = 6.283185307179586


def realify(complex_pair):
    upper_half = jnp.concatenate([complex_pair[0], -complex_pair[1]], axis=-1)
    lower_half = jnp.concatenate([complex_pair[1], complex_pair[0]], axis=-1)
    return jnp.concatenate([upper_half, lower_half], axis=-2)


def contract(form, left, right):
    return jnp.einsum(form, left, right, precision=PRECISE)


def translate(source, index, link_class, link_count, translation):
    illums = source.shape[0]
    link_slots = index.shape[0]
    spheres = index.shape[1]
    picked = jnp.take(source, index.reshape(-1), axis=2).reshape(illums, 2 * MODES, link_slots, spheres)
    slot_ids = lax.broadcasted_iota(jnp.int32, index.shape, 0)
    live_links = (slot_ids < link_count[None, :]).astype(jnp.float32)
    class_ids = lax.broadcasted_iota(jnp.int32, (OFFSETS,) + index.shape, 0)
    weights = jnp.where(class_ids == link_class[None], live_links[None], jnp.zeros_like(live_links)[None])
    binned = contract("bjks,cks->cjbs", picked, weights)
    operator_rows = jnp.transpose(realify(translation), (1, 0, 2)).reshape(2 * MODES, OFFSETS * 2 * MODES)
    translated = jnp.dot(operator_rows, binned.reshape(OFFSETS * 2 * MODES, illums * spheres), precision=PRECISE, preferred_element_type=jnp.float32)
    return translated.reshape(2 * MODES, illums, spheres)


def angles(positions, wave_ids, vertical):
    across = wave_ids[0].astype(jnp.float32)
    along = wave_ids[1].astype(jnp.float32)
    plane_angle = TWO_PI * (positions[0][:, None] * across[None, :] + positions[1][:, None] * along[None, :])
    height_angle = positions[2][:, None] * vertical[None, :]
    return plane_angle, height_angle


def expand(coefficients, positions, wave_ids, vertical, expansion):
    illums = coefficients.shape[0]
    waves = wave_ids.shape[1]
    plane_angle, height_angle = angles(positions, wave_ids, vertical)
    down_angle = plane_angle - height_angle
    phase_tiles = jnp.concatenate([jnp.cos(down_angle), jnp.sin(down_angle)], axis=1)
    products = jnp.dot(coefficients.reshape(illums * 2 * MODES, -1), phase_tiles, precision=PRECISE, preferred_element_type=jnp.float32)
    products = products.reshape(illums, 2, MODES, 2, waves)
    spec_real = products[:, 0, :, 0] + products[:, 1, :, 1]
    spec_imag = products[:, 1, :, 0] - products[:, 0, :, 1]
    out_real = contract("plw,blw->bpw", expansion[0], spec_real) - contract("plw,blw->bpw", expansion[1], spec_imag)
    out_imag = contract("plw,blw->bpw", expansion[0], spec_imag) + contract("plw,blw->bpw", expansion[1], spec_real)
    return jnp.stack([out_real, out_imag], axis=1)


def reflect(spectrum, reflection):
    spec_real = spectrum[:, 0]
    spec_imag = spectrum[:, 1]
    out_real = contract("pqw,bqw->bpw", reflection[0], spec_real) - contract("pqw,bqw->bpw", reflection[1], spec_imag)
    out_imag = contract("pqw,bqw->bpw", reflection[0], spec_imag) + contract("pqw,bqw->bpw", reflection[1], spec_real)
    return jnp.stack([out_real, out_imag], axis=1)


def wave_field(reflected, projector):
    spec_real = reflected[:, 0]
    spec_imag = reflected[:, 1]
    field_real = contract("lpw,bpw->blw", projector[0], spec_real) - contract("lpw,bpw->blw", projector[1], spec_imag)
    field_imag = contract("lpw,bpw->blw", projector[0], spec_imag) + contract("lpw,bpw->blw", projector[1], spec_real)
    return jnp.stack([field_real, field_imag], axis=1)


def up_tiles(positions, wave_ids, vertical):
    plane_angle, height_angle = angles(positions, wave_ids, vertical)
    up_angle = plane_angle + height_angle
    return jnp.concatenate([jnp.cos(up_angle), jnp.sin(up_angle)], axis=0)


def project(spectral_field, phase_tiles):
    illums = spectral_field.shape[0]
    spheres = phase_tiles.shape[0] // 2
    products = lax.dot_general(spectral_field.reshape(illums * 2 * MODES, -1), phase_tiles, (((1,), (1,)), ((), ())), precision=PRECISE, preferred_element_type=jnp.float32)
    products = products.reshape(illums, 2, MODES, 2, spheres)
    resp_real = products[:, 0, :, 0] - products[:, 1, :, 1]
    resp_imag = products[:, 0, :, 1] + products[:, 1, :, 0]
    return jnp.stack([resp_real, resp_imag], axis=1).reshape(illums, 2 * MODES, spheres)


def apply_types(exciting, sphere_type, t_matrix):
    operator_rows = realify(t_matrix).reshape(TYPES * 2 * MODES, 2 * MODES)
    all_types = jnp.dot(operator_rows, exciting.reshape(2 * MODES, -1), precision=PRECISE, preferred_element_type=jnp.float32)
    all_types = all_types.reshape(TYPES, 2 * MODES, exciting.shape[1], exciting.shape[2])
    type_ids = lax.broadcasted_iota(jnp.int32, (TYPES, exciting.shape[2]), 0)
    type_weights = (type_ids == sphere_type[None, :]).astype(jnp.float32)
    return jnp.sum(all_types * type_weights[:, None, None, :], axis=0)


def reference(coefficients, incident, positions, neighbour_index, link_class, link_count, sphere_type, translation, t_matrix, wave_grid, vertical, expansion, reflection, projector):
    translated = translate(coefficients, neighbour_index, link_class, link_count, translation)

    def blocked(array):
        leading = array.shape[:-1]
        return jnp.moveaxis(array.reshape(leading + (N_WAVE, WAVE_DEV)), -2, 0)

    def wave_block_step(summed, pieces):
        wave_ids, vertical_block, expansion_block, reflection_block, projector_block = pieces
        spectrum = expand(coefficients, positions, wave_ids, vertical_block, expansion_block)
        reflected = reflect(spectrum, reflection_block)
        phase_tiles = up_tiles(positions, wave_ids, vertical_block)
        return summed + project(wave_field(reflected, projector_block), phase_tiles), None

    start_value = jnp.zeros(coefficients.shape, jnp.float32)
    response, unused = lax.scan(wave_block_step, start_value, (blocked(wave_grid), blocked(vertical), blocked(expansion), blocked(reflection), blocked(projector)))
    exciting = jnp.transpose(incident + response, (1, 0, 2)) + translated
    return jnp.transpose(apply_types(exciting, sphere_type, t_matrix), (1, 0, 2))
```

```python
import jax
import jax.numpy as jnp
from jax import lax
from jax.sharding import PartitionSpec as P

MODES = 48
OFFSETS = 26
TYPES = 4


PRECISE = lax.Precision.HIGHEST
TWO_PI = 6.283185307179586


def with_halo(block, sides, width):
    for axis, dim in sides:
        count = lax.axis_size(axis)
        forward = [(i, i + 1) for i in range(count - 1)]
        backward = [(target, source) for source, target in forward]
        low = lax.ppermute(
            lax.slice_in_dim(block, block.shape[dim] - width, None, axis=dim), axis, forward
        )
        high = lax.ppermute(lax.slice_in_dim(block, 0, width, axis=dim), axis, backward)
        block = jnp.concatenate([low, block, high], axis=dim)
    return block


def realify(complex_pair):
    upper_half = jnp.concatenate([complex_pair[0], -complex_pair[1]], axis=-1)
    lower_half = jnp.concatenate([complex_pair[1], complex_pair[0]], axis=-1)
    return jnp.concatenate([upper_half, lower_half], axis=-2)


def contract(form, left, right):
    return jnp.einsum(form, left, right, precision=PRECISE)


def translate(source, index, link_class, link_count, translation):
    illums = source.shape[0]
    link_slots = index.shape[0]
    spheres = index.shape[1]
    flat_index = index.reshape(-1)
    source_ids = lax.broadcasted_iota(jnp.int32, (source.shape[2], flat_index.shape[0]), 0)
    chosen = (source_ids == flat_index[None, :]).astype(jnp.float32)
    picked = jnp.dot(
        source.reshape(illums * 2 * MODES, -1),
        chosen,
        precision=PRECISE,
        preferred_element_type=jnp.float32,
    ).reshape(illums, 2 * MODES, link_slots, spheres)
    slot_ids = lax.broadcasted_iota(jnp.int32, index.shape, 0)
    live_links = (slot_ids < link_count[None, :]).astype(jnp.float32)
    class_ids = lax.broadcasted_iota(jnp.int32, (OFFSETS,) + index.shape, 0)
    weights = jnp.where(
        class_ids == link_class[None], live_links[None], jnp.zeros_like(live_links)[None]
    )
    binned = contract("bjks,cks->cjbs", picked, weights)
    operator_rows = jnp.transpose(realify(translation), (1, 0, 2)).reshape(
        2 * MODES, OFFSETS * 2 * MODES
    )
    translated = jnp.dot(
        operator_rows,
        binned.reshape(OFFSETS * 2 * MODES, illums * spheres),
        precision=PRECISE,
        preferred_element_type=jnp.float32,
    )
    return translated.reshape(2 * MODES, illums, spheres)


def angles(positions, wave_ids, vertical):
    across = wave_ids[0].astype(jnp.float32)
    along = wave_ids[1].astype(jnp.float32)
    plane_angle = TWO_PI * (
        positions[0][:, None] * across[None, :] + positions[1][:, None] * along[None, :]
    )
    height_angle = positions[2][:, None] * vertical[None, :]
    return (plane_angle, height_angle)


def expand(coefficients, positions, wave_ids, vertical, expansion):
    illums = coefficients.shape[0]
    waves = wave_ids.shape[1]
    plane_angle, height_angle = angles(positions, wave_ids, vertical)
    down_angle = plane_angle - height_angle
    phase_tiles = jnp.concatenate([jnp.cos(down_angle), jnp.sin(down_angle)], axis=1)
    products = jnp.dot(
        coefficients.reshape(illums * 2 * MODES, -1),
        phase_tiles,
        precision=PRECISE,
        preferred_element_type=jnp.float32,
    )
    products = products.reshape(illums, 2, MODES, 2, waves)
    spec_real = products[:, 0, :, 0] + products[:, 1, :, 1]
    spec_imag = products[:, 1, :, 0] - products[:, 0, :, 1]
    out_real = contract("plw,blw->bpw", expansion[0], spec_real) - contract(
        "plw,blw->bpw", expansion[1], spec_imag
    )
    out_imag = contract("plw,blw->bpw", expansion[0], spec_imag) + contract(
        "plw,blw->bpw", expansion[1], spec_real
    )
    return jnp.stack([out_real, out_imag], axis=1)


def reflect(spectrum, reflection):
    spec_real = spectrum[:, 0]
    spec_imag = spectrum[:, 1]
    out_real = contract("pqw,bqw->bpw", reflection[0], spec_real) - contract(
        "pqw,bqw->bpw", reflection[1], spec_imag
    )
    out_imag = contract("pqw,bqw->bpw", reflection[0], spec_imag) + contract(
        "pqw,bqw->bpw", reflection[1], spec_real
    )
    return jnp.stack([out_real, out_imag], axis=1)


def wave_field(reflected, projector):
    spec_real = reflected[:, 0]
    spec_imag = reflected[:, 1]
    field_real = contract("lpw,bpw->blw", projector[0], spec_real) - contract(
        "lpw,bpw->blw", projector[1], spec_imag
    )
    field_imag = contract("lpw,bpw->blw", projector[0], spec_imag) + contract(
        "lpw,bpw->blw", projector[1], spec_real
    )
    return jnp.stack([field_real, field_imag], axis=1)


def up_tiles(positions, wave_ids, vertical):
    plane_angle, height_angle = angles(positions, wave_ids, vertical)
    up_angle = plane_angle + height_angle
    return jnp.concatenate([jnp.cos(up_angle), jnp.sin(up_angle)], axis=0)


def project(spectral_field, phase_tiles):
    illums = spectral_field.shape[0]
    spheres = phase_tiles.shape[0] // 2
    products = lax.dot_general(
        spectral_field.reshape(illums * 2 * MODES, -1),
        phase_tiles,
        (((1,), (1,)), ((), ())),
        precision=PRECISE,
        preferred_element_type=jnp.float32,
    )
    products = products.reshape(illums, 2, MODES, 2, spheres)
    resp_real = products[:, 0, :, 0] - products[:, 1, :, 1]
    resp_imag = products[:, 0, :, 1] + products[:, 1, :, 0]
    return jnp.stack([resp_real, resp_imag], axis=1).reshape(illums, 2 * MODES, spheres)


def apply_types(exciting, sphere_type, t_matrix):
    operator_rows = realify(t_matrix).reshape(TYPES * 2 * MODES, 2 * MODES)
    all_types = jnp.dot(
        operator_rows,
        exciting.reshape(2 * MODES, -1),
        precision=PRECISE,
        preferred_element_type=jnp.float32,
    )
    all_types = all_types.reshape(TYPES, 2 * MODES, exciting.shape[1], exciting.shape[2])
    type_ids = lax.broadcasted_iota(jnp.int32, (TYPES, exciting.shape[2]), 0)
    type_weights = (type_ids == sphere_type[None, :]).astype(jnp.float32)
    return jnp.sum(all_types * type_weights[:, None, None, :], axis=0)


def per_device(
    coefficients,
    incident,
    positions,
    neighbour_index,
    link_class,
    link_count,
    sphere_type,
    translation,
    t_matrix,
    wave_grid,
    vertical,
    expansion,
    reflection,
    projector,
):
    block_size = coefficients.shape[2]
    illums = coefficients.shape[0]
    local_index = neighbour_index - (lax.axis_index("sph") - 1) * block_size
    partial_value = expand(coefficients, positions, wave_grid, vertical, expansion)
    spectrum_share = lax.psum_scatter(partial_value, "sph", scatter_dimension=3, tiled=True)
    share_width = spectrum_share.shape[3]
    local_reflection = lax.dynamic_slice_in_dim(
        reflection, lax.axis_index("sph") * share_width, share_width, 3
    )
    reflected = lax.all_gather(reflect(spectrum_share, local_reflection), "sph", axis=3, tiled=True)
    spectral_field = wave_field(reflected, projector)
    phase_tiles = up_tiles(positions, wave_grid, vertical)
    own_count = illums // lax.axis_size("wave")
    first_illum = lax.axis_index("wave") * own_count
    own_coefs = lax.dynamic_slice_in_dim(coefficients, first_illum, own_count, 0)
    own_incident = lax.dynamic_slice_in_dim(incident, first_illum, own_count, 0)
    extended = with_halo(own_coefs, (("sph", 2),), block_size)
    translated = translate(extended, local_index, link_class, link_count, translation)
    response = lax.psum_scatter(
        project(spectral_field, phase_tiles), "wave", scatter_dimension=0, tiled=True
    )
    exciting = jnp.transpose(own_incident + response, (1, 0, 2)) + translated
    own_updated = jnp.transpose(apply_types(exciting, sphere_type, t_matrix), (1, 0, 2))
    updated = lax.all_gather(own_updated, "wave", axis=0, tiled=True)
    return updated


def solution(mesh):
    placed = (
        P(None, None, "sph"),
        P(None, None, "sph"),
        P(None, "sph"),
        P(None, "sph"),
        P(None, "sph"),
        P("sph"),
        P("sph"),
        P(),
        P(),
        P(None, "wave"),
        P("wave"),
        P(None, None, None, "wave"),
        P(None, None, None, "wave"),
        P(None, None, None, "wave"),
    )
    return jax.shard_map(
        per_device, mesh=mesh, in_specs=placed, out_specs=P(None, None, "sph"), check_vma=False
    )
```

```python
import functools
import math

import jax
import jax.numpy as jnp
from jax import lax
from jax.experimental import pallas as pl
from jax.experimental.pallas import tpu as pltpu
from jax.sharding import PartitionSpec as P

LANES = 128
MESH = pl.DeviceIdType.MESH
SIN_TERMS = [(-1) ** k * math.pi ** (2 * k + 1) / math.factorial(2 * k + 1) for k in range(6)]
COS_TERMS = [(-1) ** k * math.pi ** (2 * k) / math.factorial(2 * k) for k in range(7)]


def realify(complex_pair):
    upper_half = jnp.concatenate([complex_pair[0], -complex_pair[1]], axis=-1)
    lower_half = jnp.concatenate([complex_pair[1], complex_pair[0]], axis=-1)
    return jnp.concatenate([upper_half, lower_half], axis=-2)


def split(value):
    high = value.astype(jnp.bfloat16)
    return high, (value - high.astype(jnp.float32)).astype(jnp.bfloat16)


def dot(left, right):
    return jnp.dot(left, right, preferred_element_type=jnp.float32)


def dot3(left, right):
    return dot(left[0], right[0]) + (dot(left[0], right[1]) + dot(left[1], right[0]))


def horner(terms, x):
    total = jnp.full_like(x, terms[-1])
    for term in reversed(terms[:-1]):
        total = total * x + term
    return total


def cos_sin(turns):
    r = turns - jnp.floor(turns + 0.5)
    square = r * r
    s = r * horner(SIN_TERMS, square)
    c = horner(COS_TERMS, square)
    return 1.0 - 2.0 * (s * s), 2.0 * (s * c)


def kernel(
    n_sph, n_wave, offsets, types,
    coef_ref, inc_ref, pos_ref, index_ref, class_ref, count_ref, type_ref, op_ref, t_ref,
    grid_ref, vert_ref, exp_ref, refl_ref, proj_ref,
    out_ref,
    halo, part, part_in, spec, mirrored, up_high, up_low, picked, bin_high, bin_low, resp, resp_in,
    halo_send, halo_recv, part_send, part_recv, spec_send, spec_recv,
    resp_send, resp_recv, out_send, out_recv,
):
    me = lax.axis_index("sph")
    mine = lax.axis_index("wave")
    illums, rows, block = coef_ref.shape
    modes = rows // 2
    waves = vert_ref.shape[1]
    slots = index_ref.shape[0]
    own = illums // n_wave
    first = mine * own
    share = part.shape[1]

    barrier = pltpu.get_barrier_semaphore()
    for d in range(1, n_sph):
        pl.semaphore_signal(barrier, inc=1, device_id={"sph": lax.rem(me + d, n_sph)}, device_id_type=MESH)
    for d in range(1, n_wave):
        pl.semaphore_signal(barrier, inc=1, device_id={"wave": lax.rem(mine + d, n_wave)}, device_id_type=MESH)
    pl.semaphore_wait(barrier, n_sph + n_wave - 2)

    def halo_copy(side):
        step = 1 if side == 0 else n_sph - 1
        return pltpu.make_async_remote_copy(
            src_ref=coef_ref.at[pl.ds(first, own)],
            dst_ref=halo.at[side],
            send_sem=halo_send.at[side],
            recv_sem=halo_recv.at[side],
            device_id={"sph": lax.rem(me + step, n_sph)},
            device_id_type=MESH,
        )

    for side in range(2):
        halo_copy(side).start()

    def angles(w):
        wave = slice(w * LANES, (w + 1) * LANES)
        across = grid_ref[0:1, wave].astype(jnp.float32)
        along = grid_ref[1:2, wave].astype(jnp.float32)
        plane = pos_ref[:, 0:1] * across + pos_ref[:, 1:2] * along
        height = pos_ref[:, 2:3] * (vert_ref[:, wave] * (0.5 / math.pi))
        return plane - jnp.floor(plane + 0.5), height

    coef = split(coef_ref[...].reshape(illums * rows, block))
    for w in range(waves // LANES):
        wave = slice(w * LANES, (w + 1) * LANES)
        plane, height = angles(w)
        phases = split(jnp.concatenate(cos_sin(plane - height), axis=1))
        products = dot3(coef, phases)
        for b in range(illums):
            real = products[b * rows : b * rows + modes]
            imag = products[b * rows + modes : (b + 1) * rows]
            spec_real = real[:, :LANES] + imag[:, LANES:]
            spec_imag = imag[:, :LANES] - real[:, LANES:]
            for p in range(2):
                e_real, e_imag = exp_ref[0, p, :, wave], exp_ref[1, p, :, wave]
                sums = (e_real * spec_real - e_imag * spec_imag, e_real * spec_imag + e_imag * spec_real)
                for c in range(2):
                    row = b * 4 + c * 2 + p
                    part[row // share, row % share : row % share + 1, wave] = jnp.sum(
                        sums[c], axis=0, keepdims=True
                    )

    part_copies = []
    for d in range(1, n_sph):
        peer = lax.rem(me + d, n_sph)
        copy = pltpu.make_async_remote_copy(
            src_ref=part.at[peer],
            dst_ref=part_in.at[d],
            send_sem=part_send.at[d],
            recv_sem=part_recv.at[d],
            device_id={"sph": peer},
            device_id_type=MESH,
        )
        copy.start()
        part_copies.append(copy)

    for w in range(waves // LANES):
        wave = slice(w * LANES, (w + 1) * LANES)
        plane, height = angles(w)
        cos, sin = cos_sin(plane + height)
        high, low = split(jnp.concatenate([cos.T, sin.T], axis=1))
        up_high[wave, :] = high
        up_low[wave, :] = low

    total = part[me]
    for d, copy in enumerate(part_copies, 1):
        copy.wait_recv()
        total = total + part_in[d]
    spec[me] = total

    spec_copies = []
    for d in range(1, n_sph):
        copy = pltpu.make_async_remote_copy(
            src_ref=spec.at[me],
            dst_ref=spec.at[me],
            send_sem=spec_send.at[d],
            recv_sem=spec_recv.at[d],
            device_id={"sph": lax.rem(me + d, n_sph)},
            device_id_type=MESH,
        )
        copy.start()
        spec_copies.append(copy)

    for side in range(2):
        halo_copy(side).wait()
    around = split(
        jnp.concatenate(
            [
                halo[0].reshape(own * rows, block),
                coef_ref[pl.ds(first, own)].reshape(own * rows, block),
                halo[1].reshape(own * rows, block),
            ],
            axis=1,
        )
    )
    ids = lax.broadcasted_iota(jnp.int32, (3 * block, block), 0)
    start = (me - 1) * block
    for k in range(slots):
        chosen = jnp.where(ids == index_ref[k : k + 1, :] - start, 1.0, 0.0).astype(jnp.bfloat16)
        picked[k] = dot(around[0], chosen) + dot(around[1], chosen)

    for copy in spec_copies:
        copy.wait_recv()

    def spec_row(row):
        return spec[row // share, row % share : row % share + 1, :]

    for b in range(illums):
        real = [spec_row(b * 4 + q) for q in range(2)]
        imag = [spec_row(b * 4 + 2 + q) for q in range(2)]
        for p in range(2):
            r_real = [refl_ref[p * 2 + q : p * 2 + q + 1, :] for q in range(2)]
            r_imag = [refl_ref[4 + p * 2 + q : 5 + p * 2 + q, :] for q in range(2)]
            mirrored[b, p : p + 1, :] = sum(r_real[q] * real[q] - r_imag[q] * imag[q] for q in range(2))
            mirrored[b, 2 + p : 3 + p, :] = sum(r_real[q] * imag[q] + r_imag[q] * real[q] for q in range(2))

    up = (up_high[...], up_low[...])

    def respond(d):
        target = lax.rem(mine + d, n_wave) * own
        fields = []
        for i in range(own):
            rows_of = mirrored[target + i]
            real, imag = 0.0, 0.0
            for p in range(2):
                q_real, q_imag = proj_ref[0, p], proj_ref[1, p]
                m_real, m_imag = rows_of[p : p + 1], rows_of[2 + p : 3 + p]
                real = real + (q_real * m_real - q_imag * m_imag)
                imag = imag + (q_real * m_imag + q_imag * m_real)
            fields += [real, imag]
        products = dot3(split(jnp.concatenate(fields, axis=0)), up)
        for i in range(own):
            real = products[i * rows : i * rows + modes]
            imag = products[i * rows + modes : (i + 1) * rows]
            resp[d, i, :modes, :] = real[:, :block] - imag[:, block:]
            resp[d, i, modes:, :] = real[:, block:] + imag[:, :block]

    resp_copies = []
    for d in range(1, n_wave):
        respond(d)
        copy = pltpu.make_async_remote_copy(
            src_ref=resp.at[d],
            dst_ref=resp_in.at[d],
            send_sem=resp_send.at[d],
            recv_sem=resp_recv.at[d],
            device_id={"wave": lax.rem(mine + d, n_wave)},
            device_id_type=MESH,
        )
        copy.start()
        resp_copies.append(copy)
    respond(0)

    slot_ids = lax.broadcasted_iota(jnp.int32, (slots, block), 0)
    classes = jnp.where(slot_ids < count_ref[...], class_ref[...], -1)

    def fill(c, carry):
        binned = jnp.zeros((own * rows, block), jnp.float32)
        for k in range(slots):
            binned = binned + jnp.where(classes[k : k + 1, :] == c, picked[k], 0.0)
        high, low = split(binned)
        at = pl.ds(pl.multiple_of(c * rows, 16), rows)
        for i in range(own):
            bin_high[at, i * block : (i + 1) * block] = high[i * rows : (i + 1) * rows]
            bin_low[at, i * block : (i + 1) * block] = low[i * rows : (i + 1) * rows]
        return carry

    lax.fori_loop(0, offsets, fill, 0)
    translated = dot3(split(op_ref[...]), (bin_high[...], bin_low[...]))

    for copy in resp_copies:
        copy.wait_recv()
    exciting = []
    for i in range(own):
        value = inc_ref[first + i] + resp[0, i]
        for d in range(1, n_wave):
            value = value + resp_in[d, i]
        exciting.append(value + translated[:, i * block : (i + 1) * block])
    every = dot3(split(t_ref[...]), split(jnp.concatenate(exciting, axis=1)))
    for i in range(own):
        value = jnp.zeros((rows, block), jnp.float32)
        for t in range(types):
            value = value + jnp.where(
                type_ref[...] == t, every[t * rows : (t + 1) * rows, i * block : (i + 1) * block], 0.0
            )
        out_ref[first + i] = value

    out_copies = []
    for d in range(1, n_wave):
        copy = pltpu.make_async_remote_copy(
            src_ref=out_ref.at[pl.ds(first, own)],
            dst_ref=out_ref.at[pl.ds(first, own)],
            send_sem=out_send.at[d],
            recv_sem=out_recv.at[d],
            device_id={"wave": lax.rem(mine + d, n_wave)},
            device_id_type=MESH,
        )
        copy.start()
        out_copies.append(copy)
    for copy in part_copies + spec_copies + resp_copies:
        copy.wait_send()
    for copy in out_copies:
        copy.wait()


def per_device(
    n_sph, n_wave,
    coefficients, incident, positions, neighbour_index, link_class, link_count, sphere_type,
    translation, t_matrix, wave_grid, vertical, expansion, reflection, projector,
):
    illums, rows, block = coefficients.shape
    waves = vertical.shape[0]
    slots = neighbour_index.shape[0]
    offsets, types = translation.shape[1], t_matrix.shape[1]
    own = illums // n_wave
    share = illums * 4 // n_sph
    op_rows = jnp.transpose(realify(translation), (1, 0, 2)).reshape(rows, offsets * rows)
    t_rows = realify(t_matrix).reshape(types * rows, rows)
    args = (
        coefficients, incident, positions.T, neighbour_index, link_class, link_count.reshape(1, block),
        sphere_type.reshape(1, block), op_rows, t_rows, wave_grid, vertical.reshape(1, waves), expansion,
        reflection.reshape(8, waves), jnp.transpose(projector, (0, 2, 1, 3)),
    )
    f32, bf16 = jnp.float32, jnp.bfloat16
    sems = pltpu.SemaphoreType.DMA
    return pl.pallas_call(
        functools.partial(kernel, n_sph, n_wave, offsets, types),
        out_shape=jax.ShapeDtypeStruct(coefficients.shape, f32),
        in_specs=[pl.BlockSpec(memory_space=pltpu.VMEM)] * len(args),
        out_specs=pl.BlockSpec(memory_space=pltpu.VMEM),
        scratch_shapes=[
            pltpu.VMEM((2, own, rows, block), f32),
            pltpu.VMEM((n_sph, share, waves), f32),
            pltpu.VMEM((n_sph, share, waves), f32),
            pltpu.VMEM((n_sph, share, waves), f32),
            pltpu.VMEM((illums, 4, waves), f32),
            pltpu.VMEM((waves, 2 * block), bf16),
            pltpu.VMEM((waves, 2 * block), bf16),
            pltpu.VMEM((slots, own * rows, block), f32),
            pltpu.VMEM((offsets * rows, own * block), bf16),
            pltpu.VMEM((offsets * rows, own * block), bf16),
            pltpu.VMEM((n_wave, own, rows, block), f32),
            pltpu.VMEM((n_wave, own, rows, block), f32),
            sems((2,)), sems((2,)),
            sems((n_sph,)), sems((n_sph,)),
            sems((n_sph,)), sems((n_sph,)),
            sems((n_wave,)), sems((n_wave,)),
            sems((n_wave,)), sems((n_wave,)),
        ],
        compiler_params=pltpu.CompilerParams(
            collective_id=0, has_side_effects=True, vmem_limit_bytes=48 * 1024 * 1024
        ),
    )(*args)


def solution(mesh):
    placed = (
        P(None, None, "sph"),
        P(None, None, "sph"),
        P(None, "sph"),
        P(None, "sph"),
        P(None, "sph"),
        P("sph"),
        P("sph"),
        P(),
        P(),
        P(None, "wave"),
        P("wave"),
        P(None, None, None, "wave"),
        P(None, None, None, "wave"),
        P(None, None, None, "wave"),
    )
    return jax.shard_map(
        functools.partial(per_device, mesh.shape["sph"], mesh.shape["wave"]),
        mesh=mesh, in_specs=placed, out_specs=P(None, None, "sph"), check_vma=False,
    )
```

```python
import functools
import math

import jax
import jax.numpy as jnp
from jax import lax
from jax.experimental import pallas as pl
from jax.experimental.pallas import tpu as pltpu
from jax.sharding import PartitionSpec as P

LANES = 128
MESH = pl.DeviceIdType.MESH
SIN_TERMS = [(-1) ** k * math.pi ** (2 * k + 1) / math.factorial(2 * k + 1) for k in range(6)]
COS_TERMS = [(-1) ** k * math.pi ** (2 * k) / math.factorial(2 * k) for k in range(7)]


def realify(real, imag):
    upper_half = jnp.concatenate([real, -imag], axis=-1)
    lower_half = jnp.concatenate([imag, real], axis=-1)
    return jnp.concatenate([upper_half, lower_half], axis=-2)


def split(value):
    high = value.astype(jnp.bfloat16)
    return high, (value - high.astype(jnp.float32)).astype(jnp.bfloat16)


def dot(left, right):
    return jnp.dot(left, right, preferred_element_type=jnp.float32)


def dot3(left, right):
    return dot(left[0], right[0]) + (dot(left[0], right[1]) + dot(left[1], right[0]))


def horner(terms, x):
    total = jnp.full_like(x, terms[-1])
    for term in reversed(terms[:-1]):
        total = total * x + term
    return total


def cos_sin(turns):
    r = turns - jnp.floor(turns + 0.5)
    square = r * r
    s = r * horner(SIN_TERMS, square)
    c = horner(COS_TERMS, square)
    return 1.0 - 2.0 * (s * s), 2.0 * (s * c)


def kernel(
    n_sph, n_wave, n_args, *refs
):
    given, out_ref, here, load_sem = (
        refs[:n_args], refs[n_args], refs[n_args + 1 : 2 * n_args + 1], refs[2 * n_args + 1]
    )
    body(n_sph, n_wave, given, here, load_sem, out_ref, *refs[2 * n_args + 2 :])


def body(
    n_sph, n_wave, given, here, load_sem, out_ref,
    halo, part, part_in, spec, mirrored, up_high, up_low, picked, bin_high, bin_low, op_high, op_low, proj, resp, resp_in,
    halo_send, halo_recv, part_send, part_recv, spec_send, spec_recv,
    resp_send, resp_recv, out_send, out_recv,
):
    (
        coef_ref, pos_ref, grid_ref, vert_ref, exp_ref, index_ref, class_ref, count_ref, type_ref,
        refl_ref, proj_ref, op_ref, t_ref, inc_ref,
    ) = here
    loads = {}
    for n, (source, target) in enumerate(zip(given, here)):
        loads[id(target)] = pltpu.make_async_copy(source, target, load_sem.at[n])
        loads[id(target)].start()

    def ready(*names):
        for name in names:
            loads[id(name)].wait()

    me = lax.axis_index("sph")
    mine = lax.axis_index("wave")
    illums, rows, block = coef_ref.shape
    modes = rows // 2
    waves = vert_ref.shape[1]
    slots = index_ref.shape[0]
    own = illums // n_wave
    offsets, types = op_ref.shape[1], t_ref.shape[1]
    first = mine * own
    share = part.shape[1]

    barrier = pltpu.get_barrier_semaphore()
    for d in range(1, n_sph):
        pl.semaphore_signal(barrier, inc=1, device_id={"sph": lax.rem(me + d, n_sph)}, device_id_type=MESH)
    for d in range(1, n_wave):
        pl.semaphore_signal(barrier, inc=1, device_id={"wave": lax.rem(mine + d, n_wave)}, device_id_type=MESH)
    pl.semaphore_wait(barrier, n_sph + n_wave - 2)

    def halo_copy(side):
        step = 1 if side == 0 else n_sph - 1
        return pltpu.make_async_remote_copy(
            src_ref=given[0].at[pl.ds(first, own)],
            dst_ref=halo.at[side],
            send_sem=halo_send.at[side],
            recv_sem=halo_recv.at[side],
            device_id={"sph": lax.rem(me + step, n_sph)},
            device_id_type=MESH,
        )

    for side in range(2):
        halo_copy(side).start()

    ready(coef_ref, pos_ref, grid_ref, vert_ref, exp_ref)
    centres = jnp.concatenate(
        [pos_ref[...], jnp.zeros((block - pos_ref.shape[0], block), jnp.float32)], axis=0
    ).T

    def angles(w):
        wave = slice(w * LANES, (w + 1) * LANES)
        across = grid_ref[0:1, wave].astype(jnp.float32)
        along = grid_ref[1:2, wave].astype(jnp.float32)
        plane = centres[:, 0:1] * across + centres[:, 1:2] * along
        height = centres[:, 2:3] * (vert_ref[:, wave] * (0.5 / math.pi))
        return plane - jnp.floor(plane + 0.5), height

    coef = split(coef_ref[...].reshape(illums * rows, block))
    for w in range(waves // LANES):
        wave = slice(w * LANES, (w + 1) * LANES)
        plane, height = angles(w)
        phases = split(jnp.concatenate(cos_sin(plane - height), axis=1))
        products = dot3(coef, phases)
        for b in range(illums):
            real = products[b * rows : b * rows + modes]
            imag = products[b * rows + modes : (b + 1) * rows]
            spec_real = real[:, :LANES] + imag[:, LANES:]
            spec_imag = imag[:, :LANES] - real[:, LANES:]
            for p in range(2):
                e_real, e_imag = exp_ref[0, p, :, wave], exp_ref[1, p, :, wave]
                sums = (e_real * spec_real - e_imag * spec_imag, e_real * spec_imag + e_imag * spec_real)
                for c in range(2):
                    row = b * 4 + c * 2 + p
                    part[row // share, row % share : row % share + 1, wave] = jnp.sum(
                        sums[c], axis=0, keepdims=True
                    )

    part_copies = []
    for d in range(1, n_sph):
        peer = lax.rem(me + d, n_sph)
        copy = pltpu.make_async_remote_copy(
            src_ref=part.at[peer],
            dst_ref=part_in.at[d],
            send_sem=part_send.at[d],
            recv_sem=part_recv.at[d],
            device_id={"sph": peer},
            device_id_type=MESH,
        )
        copy.start()
        part_copies.append(copy)

    for w in range(waves // LANES):
        wave = slice(w * LANES, (w + 1) * LANES)
        plane, height = angles(w)
        cos, sin = cos_sin(plane + height)
        high, low = split(jnp.concatenate([cos.T, sin.T], axis=1))
        up_high[wave, :] = high
        up_low[wave, :] = low

    ready(proj_ref, op_ref)
    for c in range(2):
        for p in range(2):
            proj[c, p] = proj_ref[c, :, p, :]
    blank = jnp.zeros((rows, LANES - rows), jnp.float32)

    def widen(c, carry):
        high, low = split(jnp.concatenate([realify(op_ref[0, c], op_ref[1, c]), blank], axis=1))
        at = pl.ds(pl.multiple_of(c * LANES, LANES), LANES)
        op_high[:, at] = high
        op_low[:, at] = low
        return carry

    lax.fori_loop(0, offsets, widen, 0)

    total = part[me]
    for d, copy in enumerate(part_copies, 1):
        copy.wait_recv()
        total = total + part_in[d]
    spec[me] = total

    spec_copies = []
    for d in range(1, n_sph):
        copy = pltpu.make_async_remote_copy(
            src_ref=spec.at[me],
            dst_ref=spec.at[me],
            send_sem=spec_send.at[d],
            recv_sem=spec_recv.at[d],
            device_id={"sph": lax.rem(me + d, n_sph)},
            device_id_type=MESH,
        )
        copy.start()
        spec_copies.append(copy)

    ready(index_ref, class_ref, count_ref, type_ref, refl_ref, t_ref, inc_ref)
    for side in range(2):
        halo_copy(side).wait()
    around = split(
        jnp.concatenate(
            [
                halo[0].reshape(own * rows, block),
                coef_ref[pl.ds(first, own)].reshape(own * rows, block),
                halo[1].reshape(own * rows, block),
            ],
            axis=1,
        )
    )
    ids = lax.broadcasted_iota(jnp.int32, (3 * block, block), 0)
    start = (me - 1) * block
    for k in range(slots):
        chosen = jnp.where(ids == index_ref[k : k + 1, :] - start, 1.0, 0.0).astype(jnp.bfloat16)
        picked[k] = dot(around[0], chosen) + dot(around[1], chosen)

    slot_ids = lax.broadcasted_iota(jnp.int32, (slots, block), 0)
    classes = jnp.where(slot_ids < count_ref[...], class_ref[...], -1)

    def fill(c, carry):
        binned = jnp.zeros((own * rows, block), jnp.float32)
        for k in range(slots):
            binned = binned + jnp.where(classes[k : k + 1, :] == c, picked[k], 0.0)
        high, low = split(binned)
        at = pl.ds(pl.multiple_of(c * LANES, LANES), rows)
        rest = pl.ds(pl.multiple_of(c * LANES + rows, 16), LANES - rows)
        for i in range(own):
            bin_high[at, i * block : (i + 1) * block] = high[i * rows : (i + 1) * rows]
            bin_low[at, i * block : (i + 1) * block] = low[i * rows : (i + 1) * rows]
        for bins in (bin_high, bin_low):
            bins[rest, :] = jnp.zeros((LANES - rows, own * block), jnp.bfloat16)
        return carry

    lax.fori_loop(0, offsets, fill, 0)
    for copy in spec_copies:
        copy.wait_recv()

    def spec_row(row):
        return spec[row // share, row % share : row % share + 1, :]

    for b in range(illums):
        real = [spec_row(b * 4 + q) for q in range(2)]
        imag = [spec_row(b * 4 + 2 + q) for q in range(2)]
        for p in range(2):
            r_real = [refl_ref[0, p, q : q + 1, :] for q in range(2)]
            r_imag = [refl_ref[1, p, q : q + 1, :] for q in range(2)]
            mirrored[b, p : p + 1, :] = sum(r_real[q] * real[q] - r_imag[q] * imag[q] for q in range(2))
            mirrored[b, 2 + p : 3 + p, :] = sum(r_real[q] * imag[q] + r_imag[q] * real[q] for q in range(2))

    up = (up_high[...], up_low[...])

    def respond(d):
        target = lax.rem(mine + d, n_wave) * own
        fields = []
        for i in range(own):
            rows_of = mirrored[target + i]
            real, imag = 0.0, 0.0
            for p in range(2):
                q_real, q_imag = proj[0, p], proj[1, p]
                m_real, m_imag = rows_of[p : p + 1], rows_of[2 + p : 3 + p]
                real = real + (q_real * m_real - q_imag * m_imag)
                imag = imag + (q_real * m_imag + q_imag * m_real)
            fields += [real, imag]
        products = dot3(split(jnp.concatenate(fields, axis=0)), up)
        for i in range(own):
            real = products[i * rows : i * rows + modes]
            imag = products[i * rows + modes : (i + 1) * rows]
            resp[d, i, :modes, :] = real[:, :block] - imag[:, block:]
            resp[d, i, modes:, :] = real[:, block:] + imag[:, :block]

    resp_copies = []
    for d in range(1, n_wave):
        respond(d)
        for i in range(own):
            copy = pltpu.make_async_remote_copy(
                src_ref=resp.at[d, i],
                dst_ref=resp_in.at[d, i],
                send_sem=resp_send.at[d, i],
                recv_sem=resp_recv.at[d, i],
                device_id={"wave": lax.rem(mine + d, n_wave)},
                device_id_type=MESH,
            )
            copy.start()
            resp_copies.append(copy)
    respond(0)

    translated = dot3((op_high[...], op_low[...]), (bin_high[...], bin_low[...]))

    t_rows = split(
        jnp.concatenate([realify(t_ref[0, t], t_ref[1, t]) for t in range(types)], axis=0)
    )
    out_copies = []
    for i in range(own):
        value = inc_ref[first + i] + resp[0, i] + translated[:, i * block : (i + 1) * block]
        for copy in resp_copies[i::own]:
            copy.wait_recv()
        for d in range(1, n_wave):
            value = value + resp_in[d, i]
        every = dot3(t_rows, split(value))
        value = jnp.zeros((rows, block), jnp.float32)
        for t in range(types):
            value = value + jnp.where(type_ref[...] == t, every[t * rows : (t + 1) * rows], 0.0)
        out_ref[first + i] = value
        for d in range(1, n_wave):
            copy = pltpu.make_async_remote_copy(
                src_ref=out_ref.at[first + i],
                dst_ref=out_ref.at[first + i],
                send_sem=out_send.at[d, i],
                recv_sem=out_recv.at[d, i],
                device_id={"wave": lax.rem(mine + d, n_wave)},
                device_id_type=MESH,
            )
            copy.start()
            out_copies.append(copy)
    for copy in part_copies + spec_copies + resp_copies:
        copy.wait_send()
    for copy in out_copies:
        copy.wait()


def per_device(
    n_sph, n_wave,
    coefficients, incident, positions, neighbour_index, link_class, link_count, sphere_type,
    translation, t_matrix, wave_grid, vertical, expansion, reflection, projector,
):
    illums, rows, block = coefficients.shape
    waves = vertical.shape[0]
    slots = neighbour_index.shape[0]
    offsets = translation.shape[1]
    own = illums // n_wave
    share = illums * 4 // n_sph
    args = (
        coefficients, positions, wave_grid, vertical.reshape(1, waves), expansion, neighbour_index, link_class,
        link_count.reshape(1, block), sphere_type.reshape(1, block), reflection, projector, translation, t_matrix,
        incident,
    )
    f32, bf16 = jnp.float32, jnp.bfloat16
    sems = pltpu.SemaphoreType.DMA
    return pl.pallas_call(
        functools.partial(kernel, n_sph, n_wave, len(args)),
        out_shape=jax.ShapeDtypeStruct(coefficients.shape, f32),
        in_specs=[pl.BlockSpec(memory_space=pltpu.HBM)] * len(args),
        out_specs=pl.BlockSpec(memory_space=pltpu.VMEM),
        scratch_shapes=[pltpu.VMEM(a.shape, a.dtype) for a in args] + [
            sems((len(args),)),
            pltpu.VMEM((2, own, rows, block), f32),
            pltpu.VMEM((n_sph, share, waves), f32),
            pltpu.VMEM((n_sph, share, waves), f32),
            pltpu.VMEM((n_sph, share, waves), f32),
            pltpu.VMEM((illums, 4, waves), f32),
            pltpu.VMEM((waves, 2 * block), bf16),
            pltpu.VMEM((waves, 2 * block), bf16),
            pltpu.VMEM((slots, own * rows, block), f32),
            pltpu.VMEM((offsets * LANES, own * block), bf16),
            pltpu.VMEM((offsets * LANES, own * block), bf16),
            pltpu.VMEM((rows, offsets * LANES), bf16),
            pltpu.VMEM((rows, offsets * LANES), bf16),
            pltpu.VMEM((2, 2, rows // 2, waves), f32),
            pltpu.VMEM((n_wave, own, rows, block), f32),
            pltpu.VMEM((n_wave, own, rows, block), f32),
            sems((2,)), sems((2,)),
            sems((n_sph,)), sems((n_sph,)),
            sems((n_sph,)), sems((n_sph,)),
            sems((n_wave, own)), sems((n_wave, own)),
            sems((n_wave, own)), sems((n_wave, own)),
        ],
        compiler_params=pltpu.CompilerParams(
            collective_id=0, has_side_effects=True, vmem_limit_bytes=60 * 1024 * 1024
        ),
    )(*args)


def solution(mesh):
    placed = (
        P(None, None, "sph"),
        P(None, None, "sph"),
        P(None, "sph"),
        P(None, "sph"),
        P(None, "sph"),
        P("sph"),
        P("sph"),
        P(),
        P(),
        P(None, "wave"),
        P("wave"),
        P(None, None, None, "wave"),
        P(None, None, None, "wave"),
        P(None, None, None, "wave"),
    )
    return jax.shard_map(
        functools.partial(per_device, mesh.shape["sph"], mesh.shape["wave"]),
        mesh=mesh, in_specs=placed, out_specs=P(None, None, "sph"), check_vma=False,
    )
```
